32 devices in a mesh: ulysses: 4 (over x, core), blk: 8 (over z, y).
Axes of the slice: x: 2, y: 2, z: 4, core: 2. Of those that a mesh axis runs over, the one named last changes fastest.
Arguments:
- hidden_in: bfloat16 [4096, 1536], P(('ulysses', 'blk')), may hold values from -6 to 6
- out_grad: bfloat16 [4096, 1536], P(('ulysses', 'blk')), may hold values from -6 to 6
- segments: int32 [4096], replicated, may hold values from 0 to 2, as said below
- positions: int32 [4096], replicated, may hold values from 0 to 3582, as said below
- query_master: float32 [1536, 1536], P(('ulysses', 'blk')), may hold values from -0.15625 to 0.15625
- query_first: float32 [1536, 1536], P(('ulysses', 'blk')), may hold values from -9.1552734e-05 to 9.1552734e-05
- query_second: float32 [1536, 1536], P(('ulysses', 'blk')), may hold values from 1.2822512e-11 to 1.2822512e-10
- key_master: float32 [1536, 256], P(('ulysses', 'blk')), may hold values from -0.15625 to 0.15625
- key_first: float32 [1536, 256], P(('ulysses', 'blk')), may hold values from -9.1552734e-05 to 9.1552734e-05
- key_second: float32 [1536, 256], P(('ulysses', 'blk')), may hold values from 1.2822512e-11 to 1.2822512e-10
- value_master: float32 [1536, 256], P(('ulysses', 'blk')), may hold values from -0.15625 to 0.15625
- value_first: float32 [1536, 256], P(('ulysses', 'blk')), may hold values from -9.1552734e-05 to 9.1552734e-05
- value_second: float32 [1536, 256], P(('ulysses', 'blk')), may hold values from 1.2822512e-11 to 1.2822512e-10
- output_master: float32 [1536, 1536], P(None, ('ulysses', 'blk')), may hold values from -3.5 to 3.5
- output_first: float32 [1536, 1536], P(None, ('ulysses', 'blk')), may hold values from -9.1552734e-05 to 9.1552734e-05
- output_second: float32 [1536, 1536], P(None, ('ulysses', 'blk')), may hold values from 1.2822512e-11 to 1.2822512e-10
- gate_master: float32 [1536, 8960], P('blk', 'ulysses'), may hold values from -0.15625 to 0.15625
- gate_first: float32 [1536, 8960], P('blk', 'ulysses'), may hold values from -9.1552734e-05 to 9.1552734e-05
- gate_second: float32 [1536, 8960], P('blk', 'ulysses'), may hold values from 1.2822512e-11 to 1.2822512e-10
- up_master: float32 [1536, 8960], P('blk', 'ulysses'), may hold values from -0.15625 to 0.15625
- up_first: float32 [1536, 8960], P('blk', 'ulysses'), may hold values from -9.1552734e-05 to 9.1552734e-05
- up_second: float32 [1536, 8960], P('blk', 'ulysses'), may hold values from 1.2822512e-11 to 1.2822512e-10
- down_master: float32 [8960, 1536], P('ulysses', 'blk'), may hold values from -0.0625 to 0.0625
- down_first: float32 [8960, 1536], P('ulysses', 'blk'), may hold values from -9.1552734e-05 to 9.1552734e-05
- down_second: float32 [8960, 1536], P('ulysses', 'blk'), may hold values from 1.2822512e-11 to 1.2822512e-10
- small_master: float32 [5120], P(('ulysses', 'blk')), may hold values from -3 to 3
- small_first: float32 [5120], P(('ulysses', 'blk')), may hold values from -0.00036621094 to 0.00036621094
- small_second: float32 [5120], P(('ulysses', 'blk')), may hold values from 2.051602e-10 to 2.051602e-09
Outputs:
- mixed: bfloat16 [4096, 1536], P(('ulysses', 'blk'))
- input_grad: float32 [4096, 1536], P(('ulysses', 'blk'))
- grad_norm: float32 [], replicated
- query_new: float32 [1536, 1536], P(('ulysses', 'blk'))
- query_first_new: float32 [1536, 1536], P(('ulysses', 'blk'))
- query_second_new: float32 [1536, 1536], P(('ulysses', 'blk'))
- query_copy: bfloat16 [1536, 1536], P(('ulysses', 'blk'))
- key_new: float32 [1536, 256], P(('ulysses', 'blk'))
- key_first_new: float32 [1536, 256], P(('ulysses', 'blk'))
- key_second_new: float32 [1536, 256], P(('ulysses', 'blk'))
- key_copy: bfloat16 [1536, 256], P(('ulysses', 'blk'))
- value_new: float32 [1536, 256], P(('ulysses', 'blk'))
- value_first_new: float32 [1536, 256], P(('ulysses', 'blk'))
- value_second_new: float32 [1536, 256], P(('ulysses', 'blk'))
- value_copy: bfloat16 [1536, 256], P(('ulysses', 'blk'))
- output_new: float32 [1536, 1536], P(None, ('ulysses', 'blk'))
- output_first_new: float32 [1536, 1536], P(None, ('ulysses', 'blk'))
- output_second_new: float32 [1536, 1536], P(None, ('ulysses', 'blk'))
- output_copy: bfloat16 [1536, 1536], P(None, ('ulysses', 'blk'))
- gate_new: float32 [1536, 8960], P('blk', 'ulysses')
- gate_first_new: float32 [1536, 8960], P('blk', 'ulysses')
- gate_second_new: float32 [1536, 8960], P('blk', 'ulysses')
- gate_copy: bfloat16 [1536, 8960], P('blk', 'ulysses')
- up_new: float32 [1536, 8960], P('blk', 'ulysses')
- up_first_new: float32 [1536, 8960], P('blk', 'ulysses')
- up_second_new: float32 [1536, 8960], P('blk', 'ulysses')
- up_copy: bfloat16 [1536, 8960], P('blk', 'ulysses')
- down_new: float32 [8960, 1536], P('ulysses', 'blk')
- down_first_new: float32 [8960, 1536], P('ulysses', 'blk')
- down_second_new: float32 [8960, 1536], P('ulysses', 'blk')
- down_copy: bfloat16 [8960, 1536], P('ulysses', 'blk')
- small_new: float32 [5120], P(('ulysses', 'blk'))
- small_first_new: float32 [5120], P(('ulysses', 'blk'))
- small_second_new: float32 [5120], P(('ulysses', 'blk'))
- small_copy: bfloat16 [5120], P(('ulysses', 'blk'))
The draws below stay inside these ranges and needn't reach their ends.
Inputs may be any that keep to these rules, and one draw needn't show every extreme that they name: Tokens are in order: the prompt of 2048 tokens first (segment 0), then 2 continuations, segments 1 to 2, each one run of 513 to 1535 tokens. `positions`: the prompt counts from 0; each continuation counts from 2048.
All inputs are finite; a program needn't handle non-finite values.
Results may differ from the reference program's by a relative error of at most 0.019.
Values may be sent and summed in bfloat16 or wider, within the bound.
No kernel may reach another device: no remote copies, remote signals or barrier semaphores. Data moves between devices by JAX's collectives and lax.ppermute only.
A program may use at most 192 MiB of HBM per device.

```python
import math
import jax
import jax.numpy as jnp
from jax import lax

D = 1536
H = 12
KV = 2
HD = 128
FF = 8960
CONT = 1024
STEP = 10
TOKENS = 4096
NSMALL = 5120


def layout_rows(key):
    cont_total = TOKENS // (2 * CONT)
    prompt_len = TOKENS - cont_total * CONT
    pair_count = cont_total // 2
    offsets_drawn = jax.random.randint(jax.random.fold_in(key, 1), (pair_count,), 1, CONT, dtype=jnp.int32)
    if pair_count >= 2:
        offsets_drawn = offsets_drawn.at[0].set(CONT - 1)
    first_len = CONT // 2 + offsets_drawn
    second_len = CONT + CONT // 2 - offsets_drawn
    lengths = jnp.stack([first_len, second_len], 1).reshape(-1)
    lengths = jax.random.permutation(jax.random.fold_in(key, 2), lengths).astype(jnp.int32)
    starts = (prompt_len + jnp.cumsum(lengths) - lengths).astype(jnp.int32)
    row_ids = jnp.arange(TOKENS, dtype=jnp.int32)
    seg_ids = jnp.sum((row_ids[:, None] >= starts[None, :]).astype(jnp.int32), 1).astype(jnp.int32)
    table = jnp.concatenate([jnp.zeros((1,), jnp.int32), starts])
    seg_start = jnp.take(table, seg_ids).astype(jnp.int32)
    pos_ids = jnp.where(seg_ids == 0, row_ids, prompt_len + row_ids - seg_start).astype(jnp.int32)
    return (seg_ids, pos_ids)


def draw_segments(key, part):
    shared = layout_rows(key)
    return shared[0]


def draw_positions(key, part):
    shared = layout_rows(key)
    return shared[1]


def draw_small_master(key, part):
    key = jax.random.fold_in(key, 5)
    bias_key, gain_key = jax.random.split(key)
    bias_total = H * HD + 2 * KV * HD
    ramp = jnp.arange(D, dtype=jnp.float32) / D
    biases = jnp.clip(0.5 * jax.random.normal(bias_key, (bias_total,), jnp.float32), -3.0, 3.0)
    base = 0.5 + ramp
    gains = base[None, :] * jax.random.uniform(gain_key, (2, D), jnp.float32, 0.8, 1.25)
    ordered = jnp.concatenate([biases, gains.reshape(-1)])
    stored = ordered.reshape(NSMALL // (KV * HD), KV * HD).T.reshape(-1)
    return stored.astype(jnp.float32)


def block_levels(rng, dims, cuts, low, largest):
    def one(dim, blocks):
        draws = jax.random.uniform(jax.random.fold_in(jax.random.fold_in(rng, 6), dim), (blocks,), jnp.float32, low / len(cuts), largest / len(cuts))
        return jnp.repeat(jnp.exp(draws), dims[dim] // blocks).reshape((-1,) + (1,) * (len(dims) - dim - 1))

    level = one(*cuts[0])
    for cut in cuts[1:]:
        level = level * one(*cut)
    return level


def normal_values(rng, dims, spread, limit, cuts=(), kind=jnp.bfloat16):
    values = jax.random.normal(rng, dims, jnp.float32) * spread
    if len(cuts) > 0:
        values = block_levels(rng, dims, cuts, -0.22, 0.18) * values
    return jnp.clip(values, min=-limit, max=limit).astype(kind)


def setup_inputs(seed: int = 0) -> dict:
    keys = jax.random.split(jax.random.key(seed), 29)
    return {
        "hidden_in": normal_values(keys[0], (TOKENS, D), 1.0, 6.0, ((0, 32),)),
        "out_grad": normal_values(keys[1], (TOKENS, D), 1.0, 6.0, ((0, 32),)),
        "segments": draw_segments(jax.random.fold_in(keys[28], 71), 0),
        "positions": draw_positions(jax.random.fold_in(keys[28], 71), 0),
        "query_master": normal_values(keys[4], (D, H * HD), D ** -0.5, 0.15625, ((0, 32),), jnp.float32),
        "query_first": normal_values(keys[5], (D, H * HD), (0.111 * (2 * D * H * HD + 2 * D * KV * HD + 3 * D * FF) ** -0.5), 9.1552734375e-05, ((0, 32),), jnp.float32),
        "query_second": jnp.clip(jnp.exp(math.log(1.282251249623556e-10) - 2.3025851 * jax.random.uniform(keys[6], (D, H * HD), jnp.float32) ** block_levels(keys[6], (D, H * HD), ((0, 32),), -0.2, 0.2)), 1.2822512149290866e-11, 1.282251249623556e-10),
        "key_master": normal_values(keys[7], (D, KV * HD), D ** -0.5, 0.15625, ((0, 32),), jnp.float32),
        "key_first": normal_values(keys[8], (D, KV * HD), (0.111 * (2 * D * H * HD + 2 * D * KV * HD + 3 * D * FF) ** -0.5), 9.1552734375e-05, ((0, 32),), jnp.float32),
        "key_second": jnp.clip(jnp.exp(math.log(1.282251249623556e-10) - 2.3025851 * jax.random.uniform(keys[9], (D, KV * HD), jnp.float32) ** block_levels(keys[9], (D, KV * HD), ((0, 32),), -0.2, 0.2)), 1.2822512149290866e-11, 1.282251249623556e-10),
        "value_master": normal_values(keys[10], (D, KV * HD), D ** -0.5, 0.15625, ((0, 32),), jnp.float32),
        "value_first": normal_values(keys[11], (D, KV * HD), (0.111 * (2 * D * H * HD + 2 * D * KV * HD + 3 * D * FF) ** -0.5), 9.1552734375e-05, ((0, 32),), jnp.float32),
        "value_second": jnp.clip(jnp.exp(math.log(1.282251249623556e-10) - 2.3025851 * jax.random.uniform(keys[12], (D, KV * HD), jnp.float32) ** block_levels(keys[12], (D, KV * HD), ((0, 32),), -0.2, 0.2)), 1.2822512149290866e-11, 1.282251249623556e-10),
        "output_master": normal_values(keys[13], (H * HD, D), (max(1, H * HD * 8 // TOKENS)) ** -0.5, 3.5, ((1, 32),), jnp.float32),
        "output_first": normal_values(keys[14], (H * HD, D), (0.111 * (2 * D * H * HD + 2 * D * KV * HD + 3 * D * FF) ** -0.5), 9.1552734375e-05, ((1, 32),), jnp.float32),
        "output_second": jnp.clip(jnp.exp(math.log(1.282251249623556e-10) - 2.3025851 * jax.random.uniform(keys[15], (H * HD, D), jnp.float32) ** block_levels(keys[15], (H * HD, D), ((1, 32),), -0.2, 0.2)), 1.2822512149290866e-11, 1.282251249623556e-10),
        "gate_master": normal_values(keys[16], (D, FF), D ** -0.5, 0.15625, ((0, 8), (1, 4)), jnp.float32),
        "gate_first": normal_values(keys[17], (D, FF), (0.111 * (2 * D * H * HD + 2 * D * KV * HD + 3 * D * FF) ** -0.5), 9.1552734375e-05, ((0, 8), (1, 4)), jnp.float32),
        "gate_second": jnp.clip(jnp.exp(math.log(1.282251249623556e-10) - 2.3025851 * jax.random.uniform(keys[18], (D, FF), jnp.float32) ** block_levels(keys[18], (D, FF), ((0, 8), (1, 4)), -0.2, 0.2)), 1.2822512149290866e-11, 1.282251249623556e-10),
        "up_master": normal_values(keys[19], (D, FF), D ** -0.5, 0.15625, ((0, 8), (1, 4)), jnp.float32),
        "up_first": normal_values(keys[20], (D, FF), (0.111 * (2 * D * H * HD + 2 * D * KV * HD + 3 * D * FF) ** -0.5), 9.1552734375e-05, ((0, 8), (1, 4)), jnp.float32),
        "up_second": jnp.clip(jnp.exp(math.log(1.282251249623556e-10) - 2.3025851 * jax.random.uniform(keys[21], (D, FF), jnp.float32) ** block_levels(keys[21], (D, FF), ((0, 8), (1, 4)), -0.2, 0.2)), 1.2822512149290866e-11, 1.282251249623556e-10),
        "down_master": normal_values(keys[22], (FF, D), FF ** -0.5, 0.0625, ((0, 4), (1, 8)), jnp.float32),
        "down_first": normal_values(keys[23], (FF, D), (0.111 * (2 * D * H * HD + 2 * D * KV * HD + 3 * D * FF) ** -0.5), 9.1552734375e-05, ((0, 4), (1, 8)), jnp.float32),
        "down_second": jnp.clip(jnp.exp(math.log(1.282251249623556e-10) - 2.3025851 * jax.random.uniform(keys[24], (FF, D), jnp.float32) ** block_levels(keys[24], (FF, D), ((0, 4), (1, 8)), -0.2, 0.2)), 1.2822512149290866e-11, 1.282251249623556e-10),
        "small_master": draw_small_master(jax.random.fold_in(keys[28], 71), 0),
        "small_first": normal_values(keys[26], (NSMALL,), (0.444 * (2 * D * H * HD + 2 * D * KV * HD + 3 * D * FF) ** -0.5), 0.00036621094, ((0, 32),), jnp.float32),
        "small_second": jnp.clip(jnp.exp(math.log(2.0516019993976897e-09) - 2.3025851 * jax.random.uniform(keys[27], (NSMALL,), jnp.float32) ** block_levels(keys[27], (NSMALL,), ((0, 32),), -0.2, 0.2)), 2.0516019438865385e-10, 2.0516019993976897e-09),
    }


EPS = 1e-06
THETA = 1000000.0
BETA_ONE = 0.9
BETA_TWO = 0.999
ADAM_EPS = 1e-08
DECAY = 0.1
CLIP = 1.0
NEG_BIG = -1e+30
RATES = (0.03, 0.03, 0.03, 0.8, 0.03, 0.03, 0.015, 0.8)
DECAYS = (0.1, 0.1, 0.1, 0.1, 0.1, 0.1, 0.1, 0.0)

@jax.custom_vjp
def low(v):
    return lax.optimization_barrier(v.astype(jnp.bfloat16)).astype(jnp.float32)

@jax.custom_vjp
def low_back(v):
    return v

def low_keep(v):
    return (low(v), None)

def low_pass(kept, grad):
    return (grad,)

def back_keep(v):
    return (v, None)

def back_low(kept, grad):
    return (low(grad),)
low.defvjp(low_keep, low_pass)
low_back.defvjp(back_keep, back_low)

def high_dot(left, right):
    return jnp.dot(left, right, precision=lax.Precision.HIGHEST, preferred_element_type=jnp.float32)

def rope_tables(pos_rows, head_dim):
    half_dim = head_dim // 2
    frequency = THETA ** (-(jnp.arange(half_dim, dtype=jnp.float32) * 2.0 / head_dim))
    angles = pos_rows.astype(jnp.float32)[:, None] * frequency[None, :]
    cosine = jnp.cos(angles)
    sine_part = jnp.sin(angles)
    return (jnp.concatenate([cosine, cosine], -1), jnp.concatenate([sine_part, sine_part], -1))

def rotate(values, cosine, sine_part):
    half_dim = values.shape[-1] // 2
    turned = jnp.concatenate([-values[..., half_dim:], values[..., :half_dim]], -1)
    return values * cosine[:, None, :] + turned * sine_part[:, None, :]

def visible(query_seg, query_pos, key_seg, key_pos):
    same_doc = (query_seg[:, None] == key_seg[None, :]) & (key_pos[None, :] <= query_pos[:, None])
    prompt_keys = (key_seg[None, :] == 0) & (query_seg[:, None] != 0)
    return same_doc | prompt_keys

def attention(query_rot, key_rot, value_rows, segments, positions):
    block_len = min(512, TOKENS)
    block_count = TOKENS // block_len
    group = H // KV
    score_scale = HD ** (-0.5)
    queries = query_rot.reshape(block_count, block_len, KV, group, HD)
    seg_blocks = segments.reshape(block_count, block_len)
    pos_blocks = positions.reshape(block_count, block_len)

    def one_block(pieces):
        query_blk, seg_blk, pos_blk = pieces
        scores = jnp.einsum('rkgd,tkd->kgrt', query_blk, key_rot, precision=lax.Precision.HIGHEST) * score_scale
        scores = low_back(scores)
        allowed = visible(seg_blk, pos_blk, segments, positions)[None, None]
        scores = jnp.where(allowed, scores, NEG_BIG)
        row_top = lax.optimization_barrier(jnp.max(scores, -1, keepdims=True))
        weights = jnp.where(allowed, jnp.exp(scores - row_top), 0.0)
        probs = weights / lax.optimization_barrier(jnp.sum(weights, -1, keepdims=True))
        return jnp.einsum('kgrt,tkd->rkgd', low(probs), value_rows, precision=lax.Precision.HIGHEST)
    result = lax.map(jax.checkpoint(one_block), (queries, seg_blocks, pos_blocks))
    return result.reshape(TOKENS, H * HD)

def rms_normed(rows_in):
    return rows_in * lax.rsqrt(lax.optimization_barrier(jnp.mean(rows_in * rows_in, -1, keepdims=True)) + EPS)

def adam_update(master, first, second, gradient, factor, rate, decay):
    clipped = gradient * factor
    first_new = BETA_ONE * first + (1.0 - BETA_ONE) * clipped
    second_new = BETA_TWO * second + (1.0 - BETA_TWO) * clipped * clipped
    first_hat = first_new / (1.0 - BETA_ONE ** STEP)
    second_hat = second_new / (1.0 - BETA_TWO ** STEP)
    master_new = master - rate * (first_hat / (jnp.sqrt(second_hat) + ADAM_EPS) + decay * master)
    return (master_new, first_new, second_new, master_new.astype(jnp.bfloat16))

def reference(hidden_in, out_grad, segments, positions, query_master, query_first, query_second, key_master, key_first, key_second, value_master, value_first, value_second, output_master, output_first, output_second, gate_master, gate_first, gate_second, up_master, up_first, up_second, down_master, down_first, down_second, small_master, small_first, small_second):
    query_width = H * HD
    kv_width = KV * HD

    def layer(hidden, query_w, key_w, value_w, output_w, gate_w, up_w, down_w, small_w):
        w_query = low(query_w)
        w_key = low(key_w)
        w_value = low(value_w)
        w_output = low(output_w)
        w_gate = low(gate_w)
        w_up = low(up_w)
        w_down = low(down_w)
        w_small = low(small_w).reshape(kv_width, NSMALL // kv_width).T.reshape(-1)
        bias_query = w_small[:query_width]
        bias_key = w_small[query_width:query_width + kv_width]
        bias_value = w_small[query_width + kv_width:query_width + 2 * kv_width]
        gain_one = w_small[query_width + 2 * kv_width:query_width + 2 * kv_width + D]
        gain_two = w_small[query_width + 2 * kv_width + D:]
        attn_input = low(rms_normed(hidden) * gain_one)
        query_pre = low_back(high_dot(attn_input, w_query) + bias_query)
        key_pre = low_back(high_dot(attn_input, w_key) + bias_key)
        value_pre = low(low_back(high_dot(attn_input, w_value) + bias_value))
        cosine, sine_part = rope_tables(positions, HD)
        query_rot = low(low_back(rotate(query_pre.reshape(TOKENS, H, HD), cosine, sine_part)))
        key_rot = low(low_back(rotate(key_pre.reshape(TOKENS, KV, HD), cosine, sine_part)))
        attended = attention(query_rot, key_rot, value_pre.reshape(TOKENS, KV, HD), segments, positions)
        attended = low(low_back(attended))
        residual = hidden + low_back(high_dot(attended, w_output))
        ffn_input = low(rms_normed(residual) * gain_two)
        gate_value = low_back(high_dot(ffn_input, w_gate))
        up_value = low_back(high_dot(ffn_input, w_up))
        activation = low(jax.nn.silu(gate_value) * up_value)
        return residual + high_dot(activation, w_down)
    masters = (query_master, key_master, value_master, output_master, gate_master, up_master, down_master, small_master)
    firsts = (query_first, key_first, value_first, output_first, gate_first, up_first, down_first, small_first)
    seconds = (query_second, key_second, value_second, output_second, gate_second, up_second, down_second, small_second)
    result, pullback = jax.vjp(layer, hidden_in.astype(jnp.float32), *masters)
    grads = pullback(out_grad.astype(jnp.float32))
    mixed = result.astype(jnp.bfloat16)
    input_grad = grads[0]
    squares = jnp.float32(0.0)
    for gradient in grads[1:]:
        squares = squares + jnp.sum(gradient * gradient)
    grad_norm = jnp.sqrt(squares)
    factor = CLIP / jnp.maximum(grad_norm, CLIP)
    updates = [adam_update(masters[slot], firsts[slot], seconds[slot], grads[slot + 1], factor, RATES[slot], DECAYS[slot]) for slot in range(8)]
    return (mixed, input_grad, grad_norm, updates[0][0], updates[0][1], updates[0][2], updates[0][3], updates[1][0], updates[1][1], updates[1][2], updates[1][3], updates[2][0], updates[2][1], updates[2][2], updates[2][3], updates[3][0], updates[3][1], updates[3][2], updates[3][3], updates[4][0], updates[4][1], updates[4][2], updates[4][3], updates[5][0], updates[5][1], updates[5][2], updates[5][3], updates[6][0], updates[6][1], updates[6][2], updates[6][3], updates[7][0], updates[7][1], updates[7][2], updates[7][3])
```

```python
import functools
import math

import jax
import jax.numpy as jnp
from jax import lax
from jax.experimental import pallas as pl
from jax.experimental.pallas import tpu as pltpu
from jax.sharding import Mesh
from jax.sharding import PartitionSpec as P

D = 1536
H = 12
KV = 2
HD = 128
STEP = 10

EPS = 1e-06
THETA = 1000000.0
BETA_ONE = 0.9
BETA_TWO = 0.999
ADAM_EPS = 1e-08
CLIP = 1.0
NEG_BIG = -1e30
TOP_START = -1e20
RATES = (0.03, 0.03, 0.03, 0.8, 0.03, 0.03, 0.015, 0.8)
DECAYS = (0.1, 0.1, 0.1, 0.1, 0.1, 0.1, 0.1, 0.0)

ALL = ("x", "c", "z", "y")
LOG2E = 1.4426950408889634
BF = jnp.bfloat16
F32 = jnp.float32
FLIP = [(0, 1), (1, 0)]
CHUNK = 512
LONG = pl.CostEstimate(flops=32 * 10**9, bytes_accessed=2**24, transcendentals=0)
SHORT = pl.CostEstimate(flops=2**20, bytes_accessed=2**16, transcendentals=0)


def rope_tables(pos_rows, head_dim):
    half_dim = head_dim // 2
    frequency = THETA ** (-(jnp.arange(half_dim, dtype=F32) * 2.0 / head_dim))
    angles = pos_rows.astype(F32)[:, None] * frequency[None, :]
    cosine = jnp.cos(angles)
    sine_part = jnp.sin(angles)
    return (jnp.concatenate([cosine, cosine], -1), jnp.concatenate([sine_part, sine_part], -1))


def norm_forward(rows_in):
    inverse = lax.rsqrt(jnp.mean(rows_in * rows_in, -1, keepdims=True) + EPS)
    return (rows_in * inverse, inverse)


def norm_backward(upstream, normed, inverse, gains):
    scaled = upstream * gains
    inner = jnp.mean(scaled * normed, -1, keepdims=True)
    return (inverse * (scaled - normed * inner), jnp.sum(upstream * normed, 0))


def dot_nn(left, right):
    return lax.dot_general(left, right, (((1,), (0,)), ((), ())), preferred_element_type=F32)


def dot_tn(left, right):
    return lax.dot_general(left, right, (((0,), (0,)), ((), ())), preferred_element_type=F32)


def dot_nt(left, right):
    return lax.dot_general(left, right, (((1,), (1,)), ((), ())), preferred_element_type=F32)


def swap(values, axis):
    return lax.ppermute(values, axis, FLIP)


def hop(values, axes, step):
    return lax.ppermute(values, axes, [(i, i ^ step) for i in range(4)])


def trade(values, axes):
    return lax.all_to_all(values, axes, 0, 0, tiled=True)


def gather(values, axes):
    size = lax.axis_size(axes)
    return trade(jnp.broadcast_to(values[None], (size,) + values.shape), axes)


def pick(parts, index, dim=0):
    return lax.dynamic_index_in_dim(parts, index, dim, keepdims=False)


def gather_y(values):
    if lax.axis_size("y") == 2:
        return [values, swap(values, "y")]
    both = gather(values, "y")
    return [both[j] for j in range(both.shape[0])]


def y_places():
    size = lax.axis_size("y")
    return [lax.axis_index("y") ^ j if size == 2 else j for j in range(size)]


def scatter_y(parts):
    if lax.axis_size("y") == 2:
        me = lax.axis_index("y")
        return pick(parts, me).astype(F32) + swap(pick(parts, 1 - me).astype(BF), "y").astype(F32)
    return jnp.sum(trade(parts.astype(BF), "y").astype(F32), 0)


def tie(*values):
    return lax.optimization_barrier(values)


def by_place(pieces, me):
    return [lax.select_n(me ^ p, *pieces) for p in range(len(pieces))]


def spread(values):
    far = swap(values, "x")
    return [values, far, swap(values, "c"), swap(far, "c")]


def stack_heads(block, heads):
    return jnp.concatenate([block[:, h * HD : (h + 1) * HD] for h in range(heads)], 0)


def side_heads(block, heads):
    rows = block.shape[0] // heads
    return jnp.concatenate([block[h * rows : (h + 1) * rows] for h in range(heads)], 1)


def allowed_rows(qseg, qpos, kseg, kpos, heads):
    seen = ((kseg == qseg) | (kseg == 0)) & (kpos <= qpos)
    return jnp.concatenate([seen] * heads, 0)


def forward_kernel(flags, q_ref, k_ref, v_ref, w_ref, qs_ref, qp_ref, ks_ref, kp_ref, o_ref, l_ref, own_ref, oth_ref, acc, top, mass, *, heads, chunks):
    slot = pl.program_id(0)
    queries = stack_heads(q_ref[...], heads)
    qseg = qs_ref[:, 0:1]
    qpos = qp_ref[:, 0:1]
    acc[...] = jnp.zeros_like(acc)
    top[...] = jnp.full_like(top, TOP_START)
    mass[...] = jnp.zeros_like(mass)

    @pl.loop(0, chunks)
    def _(step):
        @pl.when(flags[slot, step] > 0)
        def _():
            start = pl.multiple_of(step * CHUNK, CHUNK)
            keys = k_ref[pl.ds(start, CHUNK), :]
            values = v_ref[pl.ds(start, CHUNK), :]
            kseg = ks_ref[pl.ds(step, 1), :]
            kpos = kp_ref[pl.ds(step, 1), :]
            scores = dot_nt(queries, keys) * (HD**-0.5 * LOG2E)
            scores = jnp.where(allowed_rows(qseg, qpos, kseg, kpos, heads), scores, NEG_BIG)
            old = top[:, 0:1]
            new = jnp.maximum(old, jnp.max(scores, -1, keepdims=True))
            weights = jnp.exp2(scores - new)
            shrink = jnp.exp2(old - new)
            mass[...] = mass[...] * shrink + jnp.sum(weights, -1, keepdims=True)
            acc[...] = acc[...] * shrink + dot_nn(weights.astype(BF), values)
            top[...] = jnp.broadcast_to(new, top.shape)

    outs = side_heads((acc[...] / mass[...]).astype(BF), heads)
    o_ref[...] = outs
    l_ref[0] = top[...] + jnp.log2(mass[...])
    part = dot_nt(outs, w_ref[...])

    @pl.when(slot < 2)
    def _():
        own_ref[0] = part

    @pl.when(slot >= 2)
    def _():
        oth_ref[0] = part.astype(BF)


def backward_kernel(flags, q_ref, k_ref, v_ref, w_ref, o_ref, l_ref, qs_ref, qp_ref, ks_ref, kp_ref, cos_ref, sin_ref, b0, b1, b2, b3, a0, a1, a2, a3, dq_ref, keep_ref, send_ref, wg_ref, bias_ref, acc, dk, dv, grad_rows, in_rows, gq, go, *, heads, chunks, shape):
    slot = pl.program_id(0)
    core = flags[4, 0]
    width = heads * HD

    @pl.when(slot == 0)
    def _():
        dk[...] = jnp.zeros_like(dk)
        dv[...] = jnp.zeros_like(dv)
        gq[...] = jnp.zeros_like(gq)
        go[...] = jnp.zeros_like(go)
        bias_ref[...] = jnp.zeros_like(bias_ref)

    for s, (b_ref, a_ref) in enumerate(((b0, a0), (b1, a1), (b2, a2), (b3, a3))):

        @pl.when(slot == s)
        def _():
            grad_rows[...] = b_ref[...]
            in_rows[...] = a_ref[...]

    queries = stack_heads(q_ref[...], heads)
    grads = stack_heads(dot_nn(grad_rows[...], w_ref[...]).astype(BF), heads)
    outs = stack_heads(o_ref[...], heads)
    delta = jnp.sum(grads.astype(F32) * outs.astype(F32), -1, keepdims=True)
    log_mass = l_ref[0][:, 0:1]
    qseg = qs_ref[:, 0:1]
    qpos = qp_ref[:, 0:1]
    acc[...] = jnp.zeros_like(acc)

    @pl.loop(0, chunks)
    def _(step):
        @pl.when(flags[slot, step] > 0)
        def _():
            start = pl.multiple_of(step * CHUNK, CHUNK)
            keys = k_ref[pl.ds(start, CHUNK), :]
            values = v_ref[pl.ds(start, CHUNK), :]
            kseg = ks_ref[pl.ds(step, 1), :]
            kpos = kp_ref[pl.ds(step, 1), :]
            scores = dot_nt(queries, keys) * (HD**-0.5 * LOG2E)
            seen = allowed_rows(qseg, qpos, kseg, kpos, heads)
            weights = jnp.exp2(jnp.where(seen, scores - log_mass, NEG_BIG))
            dv[pl.ds(start, CHUNK), :] += dot_tn(weights.astype(BF), grads)
            weight_grad = dot_nt(grads, values)
            score_grad = (weights * (weight_grad - delta)).astype(BF)
            acc[...] += dot_nn(score_grad, keys)
            dk[pl.ds(start, CHUNK), :] += dot_tn(score_grad, queries)

    rot_grad = (acc[...] * (HD**-0.5)).astype(BF).astype(F32)
    cosine = jnp.concatenate([cos_ref[...]] * heads, 0)
    sine_part = jnp.concatenate([sin_ref[...]] * heads, 0)
    back = rot_grad * cosine - pltpu.roll(rot_grad, HD // 2, 1) * sine_part
    query_grad = side_heads(back.astype(BF), heads)
    dq_ref[...] = query_grad
    bias_ref[...] += jnp.sum(query_grad.astype(F32), 0, keepdims=True)
    gq[...] += dot_tn(in_rows[...], query_grad)
    go[...] += dot_tn(grad_rows[...], o_ref[...])

    @pl.when(slot == 3)
    def _():
        wg_ref[:, :width] = gq[...].astype(BF)
        wg_ref[:, width:] = go[...].astype(BF)
        ny, nz, slots, tok = shape
        for s in range(slots):
            for k in range(nz):
                for j in range(ny):
                    at = ((s * nz + k) * ny + j) * tok
                    key_grad = dk[at : at + tok, :] * (HD**-0.5)
                    value_grad = dv[at : at + tok, :]
                    keep_ref[j, k, s] = jnp.where(core == 0, key_grad, value_grad)
                    send_ref[j, k, s] = jnp.where(core == 0, value_grad, key_grad).astype(BF)


def attend_specs(tok_rows, width, key_total, chunks):
    rows = pl.BlockSpec((tok_rows, width), lambda i, f: (i, 0))
    keys = pl.BlockSpec((key_total, HD), lambda i, f: (0, 0))
    row_info = pl.BlockSpec((tok_rows, 1), lambda i, f: (i, 0))
    key_info = pl.BlockSpec((chunks, CHUNK), lambda i, f: (0, 0))
    logs = pl.BlockSpec((1, width // HD * tok_rows, HD), lambda i, f: (i, 0, 0))
    weight = pl.BlockSpec((D, width), lambda i, f: (0, 0))
    return rows, keys, row_info, key_info, logs, weight


def attend_forward(flags, queries, keys, values, w_out_t, qseg, qpos, kseg, kpos, slots, heads):
    tok_rows = queries.shape[0] // slots
    key_total = keys.shape[0]
    chunks = key_total // CHUNK
    width = heads * HD
    stacked = heads * tok_rows
    rows, key_spec, row_info, key_info, logs, weight = attend_specs(tok_rows, width, key_total, chunks)
    return pl.pallas_call(
        functools.partial(forward_kernel, heads=heads, chunks=chunks),
        grid_spec=pltpu.PrefetchScalarGridSpec(
            num_scalar_prefetch=1,
            grid=(slots,),
            in_specs=[rows, key_spec, key_spec, weight, row_info, row_info, key_info, key_info],
            out_specs=[
                rows,
                logs,
                pl.BlockSpec((1, tok_rows, D), lambda i, f: (jnp.minimum(i, 1), 0, 0)),
                pl.BlockSpec((1, tok_rows, D), lambda i, f: (jnp.maximum(i - 2, 0), 0, 0)),
            ],
            scratch_shapes=[pltpu.VMEM((stacked, HD), F32)] * 3,
        ),
        out_shape=[
            jax.ShapeDtypeStruct((slots * tok_rows, width), BF),
            jax.ShapeDtypeStruct((slots, stacked, HD), F32),
            jax.ShapeDtypeStruct((2, tok_rows, D), F32),
            jax.ShapeDtypeStruct((2, tok_rows, D), BF),
        ],
        compiler_params=pltpu.CompilerParams(vmem_limit_bytes=40 * 2**20),
        cost_estimate=LONG,
        name="attend_forward",
    )(flags, queries, keys, values, w_out_t, qseg, qpos, kseg, kpos)


def attend_backward(flags, queries, keys, values, w_out_t, outs, logs_in, qseg, qpos, kseg, kpos, cosine, sine_part, grads, inputs, ny, nz, heads):
    slots = 4
    tok_rows = queries.shape[0] // slots
    key_total = keys.shape[0]
    chunks = key_total // CHUNK
    width = heads * HD
    stacked = heads * tok_rows
    rows, key_spec, row_info, key_info, logs, weight = attend_specs(tok_rows, width, key_total, chunks)
    turn = pl.BlockSpec((tok_rows, HD), lambda i, f: (i, 0))
    piece = pl.BlockSpec((tok_rows, D), lambda i, f: (0, 0))
    shape = (ny, nz, slots, tok_rows)
    split = pl.BlockSpec(shape + (HD,), lambda i, f: (0, 0, 0, 0, 0))
    return pl.pallas_call(
        functools.partial(backward_kernel, heads=heads, chunks=chunks, shape=shape),
        grid_spec=pltpu.PrefetchScalarGridSpec(
            num_scalar_prefetch=1,
            grid=(slots,),
            in_specs=[rows, key_spec, key_spec, weight, rows, logs, row_info, row_info, key_info, key_info, turn, turn]
            + [piece] * 8,
            out_specs=[
                rows,
                split,
                split,
                pl.BlockSpec((D, 2 * width), lambda i, f: (0, 0)),
                pl.BlockSpec((1, width), lambda i, f: (0, 0)),
            ],
            scratch_shapes=[
                pltpu.VMEM((stacked, HD), F32),
                pltpu.VMEM((key_total, HD), F32),
                pltpu.VMEM((key_total, HD), F32),
                pltpu.VMEM((tok_rows, D), BF),
                pltpu.VMEM((tok_rows, D), BF),
                pltpu.VMEM((D, width), F32),
                pltpu.VMEM((D, width), F32),
            ],
        ),
        out_shape=[
            jax.ShapeDtypeStruct((slots * tok_rows, width), BF),
            jax.ShapeDtypeStruct(shape + (HD,), F32),
            jax.ShapeDtypeStruct(shape + (HD,), BF),
            jax.ShapeDtypeStruct((D, 2 * width), BF),
            jax.ShapeDtypeStruct((1, width), F32),
        ],
        compiler_params=pltpu.CompilerParams(vmem_limit_bytes=60 * 2**20),
        cost_estimate=LONG,
        name="attend_backward",
    )(flags, queries, keys, values, w_out_t, outs, logs_in, qseg, qpos, kseg, kpos, cosine, sine_part, *grads, *inputs)


def project_kernel(core, a0, a1, a2, a3, w_ref, b_ref, cos_ref, sin_ref, q_ref, kv_ref, *, heads):
    tokens = jnp.concatenate([a0[...], a1[...], a2[...], a3[...]], 0)
    pre = dot_nn(tokens, w_ref[...]) + b_ref[...]
    cosine = cos_ref[...]
    sine_part = sin_ref[...]

    def turned(part):
        return part * cosine + pltpu.roll(part, HD // 2, 1) * sine_part

    for h in range(heads):
        q_ref[:, h * HD : (h + 1) * HD] = turned(pre[:, h * HD : (h + 1) * HD]).astype(BF)
    plain = pre[:, heads * HD :]
    kv_ref[...] = jnp.where(core[0] == 0, turned(plain), plain).astype(BF)


def whole_call(kernel, place, operands, outs, flops, name, scratch=()):
    return pl.pallas_call(
        kernel,
        in_specs=[pl.BlockSpec(memory_space=pltpu.SMEM)]
        + [pl.BlockSpec(memory_space=pltpu.VMEM)] * len(operands),
        out_specs=[pl.BlockSpec(memory_space=pltpu.VMEM)] * len(outs),
        out_shape=outs,
        scratch_shapes=list(scratch),
        compiler_params=pltpu.CompilerParams(vmem_limit_bytes=32 * 2**20),
        cost_estimate=SHORT,
        name=name,
    )(place, *operands)


def project(core, pieces, weights, bias, cosine, sine_part, heads):
    rows = 4 * pieces[0].shape[0]
    depth, width = weights.shape
    return whole_call(
        functools.partial(project_kernel, heads=heads),
        core,
        [*pieces, weights, bias, cosine, sine_part],
        [jax.ShapeDtypeStruct((rows, heads * HD), BF), jax.ShapeDtypeStruct((rows, HD), BF)],
        2 * rows * depth * width,
        "project",
    )


def finish_kernel(core, kv_ref, dq_ref, w_ref, cos_ref, sin_ref, a0, a1, a2, a3, own_ref, oth_ref, wg_ref, bias_ref):
    tok = a0.shape[0]
    parts = []
    for s in range(4):
        kept = kv_ref[2 * (core[0] ^ (s // 2)) + s % 2].astype(BF).astype(F32)
        cosine = cos_ref[s * tok : (s + 1) * tok, :]
        sine_part = sin_ref[s * tok : (s + 1) * tok, :]
        back = kept * cosine - pltpu.roll(kept, HD // 2, 1) * sine_part
        parts.append(jnp.where(core[0] == 0, back, kept).astype(BF))
    kv_grad = jnp.concatenate(parts, 0)
    bias_ref[...] = jnp.sum(kv_grad.astype(F32), 0, keepdims=True)
    tokens = jnp.concatenate([a0[...], a1[...], a2[...], a3[...]], 0)
    wg_ref[...] = dot_tn(tokens, kv_grad).astype(BF)
    both = jnp.concatenate([dq_ref[...], kv_grad], 1)
    in_grad = dot_nt(both, w_ref[...])
    own_ref[...] = in_grad[: 2 * tok].reshape(own_ref.shape)
    oth_ref[...] = in_grad[2 * tok :].astype(BF).reshape(oth_ref.shape)


def finish(core, kv_grad, query_grad, weights, cosine, sine_part, pieces):
    tok = pieces[0].shape[0]
    return whole_call(
        finish_kernel,
        core,
        [kv_grad, query_grad, weights, cosine, sine_part, *pieces],
        [
            jax.ShapeDtypeStruct((2, tok, D), F32),
            jax.ShapeDtypeStruct((2, tok, D), BF),
            jax.ShapeDtypeStruct((D, HD), BF),
            jax.ShapeDtypeStruct((1, HD), F32),
        ],
        8 * tok * D * (weights.shape[1] + HD),
        "finish",
    )


def unit_kernel(place, g_ref, u_ref, d_ref, pair_ref, down_ref):
    count, _, _, units = pair_ref.shape
    for k in range(count):
        low, high = k * units, (k + 1) * units
        pair_ref[k, 0] = g_ref[:, low:high].astype(BF)
        pair_ref[k, 1] = u_ref[:, low:high].astype(BF)
        down_ref[k, 0] = d_ref[:, low:high].astype(BF)


def unit_sets_of(place, gate, up, down, count):
    rows, units = gate.shape
    outs = [jax.ShapeDtypeStruct((count, n, rows, units // count), BF) for n in (2, 1)]
    return whole_call(unit_kernel, place, [gate, up, down], outs, 2**20, "unit_sets")


def assemble_kernel(places, *refs):
    whole = refs[-1]
    half = (len(refs) - 1) // 2
    for at in range(half):
        whole[0, places[at]] = refs[at][0]
        whole[1, places[at]] = refs[at][1]
        whole[2, places[at]] = refs[half + at][0]


def assemble_rows(places, pairs, downs):
    _, rows, units = pairs[0].shape
    out = jax.ShapeDtypeStruct((3, len(pairs), rows, units), BF)
    return whole_call(assemble_kernel, places, [*pairs, *downs], [out], 2**20, "assemble_rows")[0]


def ffn_kernel(place, p_ref, q_ref, cp_ref, cq_ref, y_ref, z_ref, cy_ref, g_ref, u_ref, d_ref, *rest):
    tok_ref, cot_ref, act_ref, dg_ref, du_ref, out_ref, in_own, in_oth = rest[-8:]
    step = pl.program_id(0)
    tok = p_ref.shape[0]
    near = jnp.where(step == 0, p_ref[...], cp_ref[...])
    far = jnp.where(step == 0, q_ref[...], cq_ref[...])
    first = place[1] == 0
    tokens = jnp.concatenate([jnp.where(first, near, far), jnp.where(first, far, near)], 0)
    y_near = jnp.where(step == 0, y_ref[0], cy_ref[0])
    y_far = jnp.where(step == 0, z_ref[0], cy_ref[1])
    cotangent = jnp.concatenate([jnp.where(first, y_near, y_far), jnp.where(first, y_far, y_near)], 0)
    gate_value = dot_nn(tokens, g_ref[0])
    up_value = dot_nn(tokens, u_ref[0])
    act_grad = dot_nn(cotangent, d_ref[0])
    sigmoid_gate = jax.nn.sigmoid(gate_value)
    silu_gate = gate_value * sigmoid_gate
    activation = (silu_gate * up_value).astype(BF)
    gate_grad = (
        act_grad * up_value * sigmoid_gate * (1.0 + gate_value * (1.0 - sigmoid_gate))
    ).astype(BF)
    up_grad = (act_grad * silu_gate).astype(BF)
    tok_ref[...] = tokens.reshape(tok_ref.shape)
    cot_ref[...] = cotangent.reshape(cot_ref.shape)
    act_ref[...] = activation.reshape(act_ref.shape)
    dg_ref[...] = gate_grad.reshape(dg_ref.shape)
    du_ref[...] = up_grad.reshape(du_ref.shape)
    out_ref[...] = dot_nt(activation, d_ref[0]).astype(BF).reshape(out_ref.shape)
    in_part = (dot_nt(gate_grad, g_ref[0]) + dot_nt(up_grad, u_ref[0])).astype(BF)
    low, high = in_part[:tok], in_part[tok:]

    def put(ref):
        ref[0] = jnp.where(first, low, high)
        ref[1] = jnp.where(first, high, low)

    @pl.when(step == 0)
    def _():
        put(in_own)

    @pl.when(step == 1)
    def _():
        put(in_oth)


def ffn_piece(place, pieces, cotangents, weights, kept):
    tok = pieces[0].shape[0]
    nz = cotangents[0].shape[0]
    units = weights.shape[-1]

    def here(width):
        return pl.BlockSpec((1, 2, 1, tok, width), lambda i, p: (i ^ p[0], 0, p[2], 0, 0))

    def matrix(at):
        return pl.BlockSpec((1, D, units), lambda i, p: (at, 0, 0))

    piece = pl.BlockSpec((tok, D), lambda i, p: (0, 0))
    cotangent = pl.BlockSpec((1, tok, D), lambda i, p: (p[2], 0, 0))
    in_spec = pl.BlockSpec((2, tok, D), lambda i, p: (0, 0, 0))
    wide = jax.ShapeDtypeStruct((2, 2, nz, tok, D), BF)
    thin = jax.ShapeDtypeStruct((2, 2, nz, tok, units), BF)
    operands = [*pieces, *cotangents, weights, weights, weights, *kept]
    results = pl.pallas_call(
        ffn_kernel,
        grid_spec=pltpu.PrefetchScalarGridSpec(
            num_scalar_prefetch=1,
            grid=(2,),
            in_specs=[piece] * 4
            + [cotangent, cotangent, in_spec, matrix(0), matrix(1), matrix(2)]
            + [pl.BlockSpec(memory_space=pl.ANY)] * len(kept),
            out_specs=[here(D), here(D), here(units), here(units), here(units), here(D), in_spec, in_spec],
        ),
        out_shape=[wide, wide, thin, thin, thin, wide]
        + [jax.ShapeDtypeStruct((2, tok, D), BF)] * 2,
        input_output_aliases={11 + i: i for i in range(len(kept))},
        compiler_params=pltpu.CompilerParams(vmem_limit_bytes=44 * 2**20),
        cost_estimate=LONG,
        name="ffn_piece",
    )(place, *operands)
    return results[:6], results[6], results[7]


def weight_kernel(place, t_ref, y_ref, a_ref, g_ref, u_ref, *outs):
    half = outs[0].shape[1]
    first = place[0] == 0
    for at, (left, right) in enumerate(((t_ref, g_ref), (t_ref, u_ref), (y_ref, a_ref))):
        grad = dot_tn(left[...], right[...]).astype(BF)
        outs[2 * at][0] = jnp.where(first, grad[:half], grad[half:])
        outs[2 * at + 1][0] = jnp.where(first, grad[half:], grad[:half])


def weight_grads(place, tokens, cotangents, act, gate_grad, up_grad, nz):
    rows = tokens.shape[0]
    units = act.shape[1]
    depth = D // nz
    wide = pl.BlockSpec((rows, depth), lambda i, p: (0, i))
    thin = pl.BlockSpec((rows, units), lambda i, p: (0, 0))
    out = pl.BlockSpec((1, depth // 2, units), lambda i, p: (i, 0, 0))
    return pl.pallas_call(
        weight_kernel,
        grid_spec=pltpu.PrefetchScalarGridSpec(
            num_scalar_prefetch=1,
            grid=(nz,),
            in_specs=[wide, wide, thin, thin, thin],
            out_specs=[out] * 6,
        ),
        out_shape=[jax.ShapeDtypeStruct((nz, depth // 2, units), BF)] * 6,
        compiler_params=pltpu.CompilerParams(vmem_limit_bytes=48 * 2**20),
        cost_estimate=LONG,
        name="weight_grads",
    )(place, tokens, cotangents, act, gate_grad, up_grad)


def adam_update(master, first, second, gradient, factor, rate, decay):
    clipped = gradient * factor
    first_new = BETA_ONE * first + (1.0 - BETA_ONE) * clipped
    second_new = BETA_TWO * second + (1.0 - BETA_TWO) * clipped * clipped
    first_hat = first_new / (1.0 - BETA_ONE**STEP)
    second_hat = second_new / (1.0 - BETA_TWO**STEP)
    master_new = master - rate * (first_hat / (jnp.sqrt(second_hat) + ADAM_EPS) + decay * master)
    return (master_new, first_new, second_new, master_new.astype(BF))


def body(
    hidden_in,
    out_grad,
    segments,
    positions,
    query_master,
    query_first,
    query_second,
    key_master,
    key_first,
    key_second,
    value_master,
    value_first,
    value_second,
    output_master,
    output_first,
    output_second,
    gate_master,
    gate_first,
    gate_second,
    up_master,
    up_first,
    up_second,
    down_master,
    down_first,
    down_second,
    small_master,
    small_first,
    small_second,
):
    nx, nc, nz, ny = (lax.axis_size(a) for a in ALL)
    ix, ic, iz, iy = (lax.axis_index(a) for a in ALL)
    nu = nx * nc
    nb = nz * ny
    me_u = ix * nc + ic
    me_b = iz * ny + iy
    tok = hidden_in.shape[0]
    qw = H * HD
    kvw = KV * HD
    heads = H // nu
    hw = heads * HD
    pack = hw + HD + hw
    rows_w = query_master.shape[0]

    q_cols = query_master.astype(BF).reshape(rows_w, nu, hw)
    k_cols = key_master.astype(BF).reshape(rows_w, nx, 1, HD)
    v_cols = value_master.astype(BF).reshape(rows_w, nx, 1, HD)
    kv_cols = jnp.concatenate([k_cols, v_cols], 2).reshape(rows_w, nu, HD)
    o_cols = output_master.astype(BF).T.reshape(rows_w, nu, hw)
    y_at = y_places()
    packed = trade(
        jnp.transpose(jnp.concatenate([q_cols, kv_cols, o_cols], -1), (1, 0, 2)), ("x", "c")
    )
    packed, small_bf, hidden_in = tie(packed, small_master.astype(BF), hidden_in)
    core = jnp.reshape(ic, (1,)).astype(jnp.int32)
    own_qkv = packed[:, :, : hw + HD]
    own_out = packed[:, :, hw + HD :]
    qkv_far = [own_qkv] + [hop(own_qkv, "z", k) for k in range(1, nz)]
    small_all = gather(small_bf, ALL).reshape(-1)

    def assemble(pieces, lead):
        whole = None
        for k, along in enumerate(pieces):
            for place, part in zip(y_at, along):
                shape = part.shape[:lead] + (1, 1) + part.shape[lead:]
                if whole is None:
                    whole = jnp.zeros(part.shape[:lead] + (nz, ny) + part.shape[lead:], BF)
                at = (0,) * lead + (iz ^ k, place) + (0,) * (part.ndim - lead)
                whole = lax.dynamic_update_slice(whole, part.reshape(shape), at)
        return whole

    qkv_far[1], qkv_far[2], qkv_far[3], out_grad, gate_master, up_master, down_rows = tie(
        *qkv_far[1:], out_grad, gate_master, up_master, down_master.T
    )
    grad_near = lax.all_gather(out_grad, "z")
    pair_sets, down_sets = unit_sets_of(core, gate_master, up_master, down_rows, nz)
    pair_all = [gather_y(pick(pair_sets, iz))]
    down_all = [gather_y(pick(down_sets, iz))]
    w_qkv = assemble([gather_y(far) for far in qkv_far], 1).reshape(D, hw + HD)


    small_vals = small_all.astype(F32).reshape(kvw, -1).T.reshape(-1)
    bias_qkv = jnp.concatenate(
        [
            lax.dynamic_slice_in_dim(small_vals, me_u * hw, hw),
            lax.dynamic_slice_in_dim(small_vals, qw + ic * kvw + ix * HD, HD),
        ]
    )
    gain_one = small_vals[qw + 2 * kvw : qw + 2 * kvw + D]
    gain_two = small_vals[qw + 2 * kvw + D :]

    slot_u = jnp.stack([(ix ^ a) * nc + (ic ^ b) for b in range(2) for a in range(2)])
    key_u = jnp.stack([(ix ^ a) * nc + b for b in range(2) for a in range(2)])
    key_b = jnp.stack([(iz ^ k) * ny + place for k in range(nz) for place in y_at])
    seg_grid = segments.reshape(nu, nb, tok)
    pos_grid = positions.reshape(nu, nb, tok)
    qseg = jnp.take(pick(seg_grid, me_b, 1), slot_u, 0)
    qpos = jnp.take(pick(pos_grid, me_b, 1), slot_u, 0)
    kseg = jnp.take(jnp.take(seg_grid, key_u, 0), key_b, 1).reshape(-1, CHUNK)
    kpos = jnp.take(jnp.take(pos_grid, key_u, 0), key_b, 1).reshape(-1, CHUNK)
    key_start = (key_u[:, None] * nb + key_b[None, :]) * tok
    key_first_index = jnp.min(key_start.reshape(-1, CHUNK // tok), -1)
    query_last_index = (slot_u * nb + me_b) * tok + tok - 1
    kseg_low, kseg_high = jnp.min(kseg, -1), jnp.max(kseg, -1)
    qseg_low, qseg_high = jnp.min(qseg, -1), jnp.max(qseg, -1)
    flags = (
        (key_first_index[None, :] <= query_last_index[:, None])
        & (
            (kseg_low[None, :] == 0)
            | (
                (kseg_low[None, :] <= qseg_high[:, None])
                & (qseg_low[:, None] <= kseg_high[None, :])
            )
        )
    ).astype(jnp.int32)
    qseg = qseg.reshape(-1, 1)
    qpos = qpos.reshape(-1, 1)
    half = HD // 2
    cosine, sine_part = rope_tables(qpos[:, 0], HD)
    sine_part = jnp.where(jnp.arange(HD)[None, :] < half, -sine_part, sine_part)

    def home(own, oth):
        came = swap(oth, "c")
        far = (own[1].astype(F32) + came[1].astype(F32)).astype(BF)
        far = swap(far, "x")
        return own[0].astype(F32) + came[0].astype(F32) + far.astype(F32), came, far

    hidden = hidden_in.astype(F32)
    normed_one, inverse_one = norm_forward(hidden)
    attn_input = spread((normed_one * gain_one).astype(BF))
    attn_input[0], grad_near = tie(attn_input[0], grad_near)
    grad_far = swap(grad_near, "x")
    queries, kv_own = project(core, attn_input, w_qkv, bias_qkv[None, :], cosine, sine_part, heads)

    def core_order(values):
        split = values.reshape(2, -1, values.shape[-1])
        return jnp.where(ic == 0, split, split[::-1]).reshape(values.shape)

    kv_own = core_order(kv_own)
    kv_far = [kv_own] + [hop(kv_own, "z", k) for k in range(1, nz)]
    kv_near = jnp.stack([far.reshape(nu, tok, HD) for far in kv_far], 1)
    kv_near, own_out, pair_sets, pair_all[0], down_all[0] = tie(
        kv_near, own_out, pair_sets, pair_all[0], down_all[0]
    )
    out_far = [own_out] + [hop(own_out, "z", k) for k in range(1, nz)]
    pair_far = [hop(pick(pair_sets, iz ^ k), "z", k) for k in range(1, nz)]
    kv_mine = jnp.stack(gather_y(kv_near), 2).reshape(-1, HD)
    kv_mine, *out_far[1:] = tie(kv_mine, *out_far[1:])
    w_out_t = assemble([gather_y(far) for far in out_far], 1).reshape(D, hw)
    kv_other = swap(kv_mine, "c")
    kv_other, down_sets, grad_far, *pair_far = tie(kv_other, down_sets, grad_far, *pair_far)
    pair_all += [gather_y(pair_far[0]), gather_y(pair_far[1])]
    down_far = [hop(pick(down_sets, iz ^ k), "z", k) for k in range(1, nz)]
    key_all = jnp.where(ic == 0, kv_mine, kv_other)
    value_all = jnp.where(ic == 0, kv_other, kv_mine)

    unit_places = jnp.stack([(iz ^ k) * ny + place for k in range(nz) for place in y_at])
    attended, logs, part_own, part_oth = attend_forward(
        flags, queries, key_all, value_all, w_out_t, qseg, qpos, kseg, kpos, nu, heads
    )
    part_oth, pair_all[1], pair_all[2], *down_far = tie(
        part_oth, pair_all[1], pair_all[2], *down_far
    )
    pair_all.append(gather_y(pair_far[2]))
    down_all += [gather_y(far) for far in down_far]
    part_came = swap(part_oth, "c")
    branch_far = swap((part_own[1] + part_came[1].astype(F32)).astype(BF), "x")
    branch = part_own[0] + part_came[0].astype(F32) + branch_far.astype(F32)
    residual = hidden + branch
    normed_two, inverse_two = norm_forward(residual)
    ffn_input = (normed_two * gain_two).astype(BF)
    near_x, near_c = swap(ffn_input, "x"), swap(ffn_input, "c")
    tok_far = [ffn_input] + [hop(ffn_input, "z", k) for k in range(1, nz)]
    tok_far[1], tok_far[2], tok_far[3], grad_far, pair_all[3], *down_all[1:] = tie(
        *tok_far[1:], grad_far, pair_all[3], *down_all[1:]
    )
    ffn_weights = assemble_rows(
        unit_places.astype(jnp.int32),
        [part for along in pair_all for part in along],
        [part for along in down_all for part in along],
    ).reshape(3, D, -1)
    pairs = [jnp.stack([pick(grad_near, iz ^ k), pick(grad_far, iz ^ k)]) for k in range(nz)]
    pairs = [swap(pair, "c") for pair in pairs]
    kept, came, far, owns = [], [], [], []
    last = nz - 1
    tok_far[0], tok_far[1], tok_far[2], tok_far[3] = tie(*tok_far)
    pieces = [[tok_far[0], near_x, near_c]]
    pieces += [[values, swap(values, "x"), swap(values, "c")] for values in tok_far[1:]]
    for k in range(nz):
        spot = jnp.stack([ic, ix, iz ^ k]).astype(jnp.int32)
        both = swap(pieces[k][1], "c")
        if k > 0:
            both, came[k - 1] = tie(both, came[k - 1])
        kept, in_own, in_oth = ffn_piece(
            spot, pieces[k] + [both], [grad_near, grad_far, pairs[k]], ffn_weights, kept
        )
        if k < last:
            in_oth, pairs[k + 1], *pieces[k + 1][1:] = tie(in_oth, pairs[k + 1], *pieces[k + 1][1:])
        if 0 < k < last:
            in_oth, far[k - 1] = tie(in_oth, far[k - 1])
        owns.append(in_own.astype(F32))
        came.append(swap(in_oth, "c"))
        far.append(swap((owns[k][1] + came[k][1].astype(F32)).astype(BF), "x"))
    backs = []
    for k in range(nz):
        back = owns[k][0] + came[k][0].astype(F32) + far[k].astype(F32)
        backs.append(back if k == 0 else hop(back.astype(BF), "z", k))
    tokens_all, cotangent_all, act_all, gate_all, up_all, out_all = kept
    out_sum = lax.psum_scatter(out_all, "c", scatter_dimension=0)
    tokens_all, far[last], out_sum = tie(tokens_all, far[last], out_sum)
    out_sum = lax.psum_scatter(out_sum, "x", scatter_dimension=0)
    units = act_all.shape[-1]
    halves = weight_grads(
        jnp.reshape(iy if ny == 2 else 0 * iy, (1,)).astype(jnp.int32),
        tokens_all.reshape(-1, D),
        cotangent_all.reshape(-1, D),
        act_all.reshape(-1, units),
        gate_all.reshape(-1, units),
        up_all.reshape(-1, units),
        nz,
    )
    halves = list(halves)
    backs[last], halves[0] = tie(backs[last], halves[0])
    ffn_in_grad = backs[0] + backs[1].astype(F32) + backs[2].astype(F32) + backs[3].astype(F32)
    norm_two_grad, gain_two_grad = norm_backward(ffn_in_grad, normed_two, inverse_two, gain_two)
    residual_grad = out_grad.astype(F32) + norm_two_grad

    def near_parts(mine, other):
        if ny == 2:
            return mine, swap(other, "y")
        both = jnp.concatenate([mine, other], 1).reshape(nz, ny, -1, units)
        return scatter_y(jnp.moveaxis(both, 1, 0)).astype(BF), None

    def near_pieces(mine, sent):
        parts = [pick(mine, iz ^ k) for k in range(nz)]
        if sent is None:
            return parts
        came = [pick(sent, iz ^ k) for k in range(nz)]
        return [(a.astype(F32) + b.astype(F32)).astype(BF) for a, b in zip(parts, came)]

    def units_side(pieces):
        return jnp.concatenate([pieces[k] for k in range(nz)], -1)

    gate_mine, gate_sent = near_parts(*halves[0:2])
    up_mine, up_sent = near_parts(*halves[2:4])
    down_mine, down_sent = near_parts(*halves[4:6])

    def heads_near(parts):
        split = jnp.transpose(parts.reshape(nu, nz, ny, rows_w, parts.shape[-1]), (2, 1, 0, 3, 4))
        return scatter_y(split)

    def heads_sum(split):
        total = pick(split, iz)
        for k in range(1, nz):
            total = total + hop(pick(split, iz ^ k).astype(BF), "z", k).astype(F32)
        return total

    branch_grad = spread(residual_grad.astype(BF))
    branch_grad[1], gate_mine = tie(branch_grad[1], gate_mine)
    gate_near = near_pieces(gate_mine, gate_sent)
    branch_grad[3], out_sum, *gate_near = tie(branch_grad[3], out_sum, *gate_near)
    out_sum = lax.psum_scatter(out_sum, "z", scatter_dimension=0)

    def units_home(pieces):
        return pieces[:1] + [hop(pieces[k], "z", k) for k in range(1, nz)]

    gate_home = units_home(gate_near)

    core_flags = jnp.concatenate([flags, jnp.full((1, flags.shape[1]), ic, jnp.int32)], 0)
    query_grad, kv_keep, kv_send, qo_grad, bias_q_grad = attend_backward(
        core_flags, queries, key_all, value_all, w_out_t, attended, logs, qseg, qpos, kseg, kpos,
        cosine, sine_part, branch_grad, attn_input, ny, nz, heads
    )
    kv_send, up_sent, down_sent, out_sum, *gate_home = tie(
        kv_send, up_sent, down_sent, out_sum, *gate_home
    )
    kv_came = swap(kv_send, "c")
    up_home = units_home(near_pieces(up_mine, up_sent))
    if ny == 2:
        kv_other = (kv_keep[1] + kv_came[1].astype(F32)).astype(BF)
        kv_other = swap(kv_other, "y")
        kv_other, qo_grad = tie(kv_other, qo_grad)
        kv_sum = kv_keep[0] + kv_came[0].astype(F32) + kv_other.astype(F32)
    else:
        kv_sum = scatter_y(kv_keep + kv_came.astype(F32))
    kv_grad = kv_sum[0]
    for k in range(1, nz):
        kv_grad = kv_grad + hop(kv_sum[k].astype(BF), "z", k).astype(F32)
    qo_near = heads_near(qo_grad)
    kv_grad, qo_near, down_sent = tie(kv_grad, qo_near, down_sent)
    down_home = units_home(near_pieces(down_mine, down_sent))
    in_own, in_oth, kv_w_grad, bias_kv_grad = finish(
        core, kv_grad, query_grad, w_qkv, cosine, sine_part, attn_input
    )
    in_oth, *gate_home = tie(in_oth, *gate_home)
    attn_in_grad, _, attn_far = home(in_own, in_oth)
    norm_one_grad, gain_one_grad = norm_backward(attn_in_grad, normed_one, inverse_one, gain_one)
    input_grad = residual_grad + norm_one_grad

    kv_w_grad, *up_home = tie(kv_w_grad, *up_home)
    kv_near = heads_near(kv_w_grad)
    total = jnp.concatenate([heads_sum(qo_near), heads_sum(kv_near)], -1).astype(BF)
    total = trade(total, ("x", "c"))
    total, attn_far, *down_home = tie(total, attn_far, *down_home)
    mixed = (residual + out_sum.astype(F32)).astype(BF)
    g_query = jnp.concatenate([total[u, :, :hw] for u in range(nu)], -1)
    g_output = jnp.concatenate([total[u, :, hw : 2 * hw] for u in range(nu)], -1).T
    g_key = jnp.concatenate([total[u, :, 2 * hw :] for u in range(0, nu, 2)], -1)
    g_value = jnp.concatenate([total[u, :, 2 * hw :] for u in range(1, nu, 2)], -1)


    bias_q_grad, bias_kv_grad = bias_q_grad[0], bias_kv_grad[0]
    bias_all = lax.dynamic_update_slice_in_dim(
        jnp.zeros((qw + 2 * kvw,), F32), bias_q_grad, me_u * hw, 0
    )
    bias_all = lax.dynamic_update_slice_in_dim(
        bias_all, bias_kv_grad, qw + ic * kvw + ix * HD, 0
    )
    small_ordered = jnp.concatenate([bias_all, gain_one_grad, gain_two_grad])
    small_grad = small_ordered.reshape(-1, kvw).T.reshape(nu * nb, -1)
    g_small = jnp.sum(trade(small_grad, ALL), 0)
    g_query, g_key, g_value, g_output = (
        lax.optimization_barrier(g).astype(F32) for g in (g_query, g_key, g_value, g_output)
    )
    local_squares = jnp.float32(0.0)
    for part in (g_query, g_key, g_value, g_output, g_small, *gate_home, *up_home, *down_home):
        wide = part.astype(F32)
        local_squares = local_squares + jnp.sum(wide * wide)
    homes = gate_home + up_home + list(down_home)
    local_squares, mixed, *homes = tie(local_squares, mixed, *homes)
    g_gate, g_up, g_down = (
        lax.optimization_barrier(units_side(by_place(homes[at : at + nz], iz)))
        for at in (0, nz, 2 * nz)
    )
    g_gate, g_up, g_down = g_gate.astype(F32), g_up.astype(F32), g_down.T.astype(F32)
    shards = (g_query, g_key, g_value, g_output, g_gate, g_up, g_down, g_small)
    squares = trade(jnp.full((nu * nb, HD), local_squares, F32), ALL)
    grad_norm = jnp.sqrt(jnp.sum(squares[:, 0]))
    factor = CLIP / jnp.maximum(grad_norm, CLIP)
    masters = (query_master, key_master, value_master, output_master, gate_master, up_master, down_master, small_master)
    firsts = (query_first, key_first, value_first, output_first, gate_first, up_first, down_first, small_first)
    seconds = (query_second, key_second, value_second, output_second, gate_second, up_second, down_second, small_second)
    results = [mixed, input_grad, grad_norm]
    for slot in range(8):
        results.extend(
            adam_update(
                masters[slot],
                firsts[slot],
                seconds[slot],
                shards[slot],
                factor,
                RATES[slot],
                DECAYS[slot],
            )
        )
    return tuple(results)


def solution(mesh):
    ulysses, blk = mesh.devices.shape
    fine = Mesh(mesh.devices.reshape(2, ulysses // 2, 4, blk // 4), ALL)
    rows = P(ALL, None)
    cols = P(None, ALL)
    wide = P(("z", "y"), ("x", "c"))
    tall = P(("x", "c"), ("z", "y"))
    flat = P(ALL)
    in_specs = (rows, rows, P(), P()) + (rows,) * 9 + (cols,) * 3 + (wide,) * 6 + (tall,) * 3 + (flat,) * 3
    out_specs = (rows, rows, P()) + (rows,) * 12 + (cols,) * 4 + (wide,) * 8 + (tall,) * 4 + (flat,) * 4
    return jax.shard_map(body, mesh=fine, in_specs=in_specs, out_specs=out_specs, check_vma=False)
```
